32 devices in a mesh: groups: 2 (over x), row: 16 (over z, y, core).
Axes of the slice: x: 2, y: 2, z: 4, core: 2. Of those that a mesh axis runs over, the one named last changes fastest.
Arguments:
- gate_pre: bfloat16 [1024, 32768], P('groups', 'row'), parts along dimension 0, may hold values from -6 to 6
- up_pre: bfloat16 [1024, 32768], P('groups', 'row'), parts along dimension 0, may hold values from -6 to 6
- residual: bfloat16 [1024, 8192], P('groups', 'row'), parts along dimension 0, may hold values from -32 to 32
- gain: float32 [8192], replicated, may hold values from 0.5 to 1.5
- down_weight: bfloat16 [131072, 2048], P('row'), may hold values from -0.046875 to 0.046875
Outputs:
- mixed: bfloat16 [1024, 8192], P('groups', 'row'), parts along dimension 0
- normed: bfloat16 [1024, 8192], P('groups', 'row'), parts along dimension 0
The draws below stay inside these ranges and needn't reach their ends.
There are 2 independent parts, one for each index of `groups`. The reference program is written for one: setup_inputs(seed, part) draws one part's arguments, and reference() takes and returns one part's arrays. A program takes and returns all parts, laid end to end along the dimension named above; an argument that names none is the same for every part. Nothing has to cross between parts.
All inputs are finite; a program needn't handle non-finite values.
Results may differ from the reference program's by a relative error of at most 0.0028.
Values may be sent and summed in bfloat16 or wider, within the bound.
No kernel may reach another device: no remote copies, remote signals or barrier semaphores. Data moves between devices by JAX's collectives and lax.ppermute only.
A program may use at most 256 MiB of HBM per device.

```python
import jax
import jax.numpy as jnp
from jax import lax

D = 8192
FF = 32768
QUAD = 4
TOKENS = 512
N_ROW = 16


def draw_residual(key, part):
    key = jax.random.fold_in(key, 11)
    first, second, third = jax.random.split(key, 3)
    column = jnp.arange(D, dtype=jnp.float32) / D
    column_scale = 10.0 ** (0.5 * column + 0.5 * jax.random.uniform(second, (D,), jnp.float32))
    row_scale = 10.0 ** (0.5 * jax.random.uniform(third, (TOKENS, 1), jnp.float32))
    base = jnp.clip(jax.random.normal(first, (TOKENS, D), jnp.float32), -4.0, 4.0)
    values = 0.25 * base * row_scale * column_scale[None, :]
    return values.astype(jnp.bfloat16)


def strengthened(values, own_key, source, target, parts, factor):
    owner, partner = [(jnp.arange(values.shape[position]) // (values.shape[position] // parts)).reshape([-1 if axis == position else 1 for axis in range(values.ndim)]) for position in (source, target)]
    chosen = jax.random.permutation(own_key, parts)[partner]
    strong = (owner == chosen) | (owner == (partner + parts // 2) % parts)
    return jnp.where(strong, factor * values, values)


def levels(own_key, extent, cuts, least, high):
    level, own = 1.0, jax.random.fold_in(own_key, 6)
    for axis_at, blocks in cuts:
        heights = jnp.exp(jax.random.uniform(jax.random.fold_in(own, axis_at), (blocks,), jnp.float32, least / len(cuts), high / len(cuts)))
        level = level * jnp.repeat(heights, extent[axis_at] // blocks).reshape([-1 if axis == axis_at else 1 for axis in range(len(extent))])
    return level


def noise(stream_key, extent, width, most, shards=(), kind=jnp.bfloat16):
    level = levels(stream_key, extent, shards, -0.22, 0.18) if shards else 1.0
    array = jax.random.normal(stream_key, extent, jnp.float32) * width * level
    return jnp.minimum(jnp.maximum(array, -most), most).astype(kind)


def gaussian_with(key, extent, scale, reach, pieces, heavy, kind=jnp.bfloat16):
    result = scale * jax.random.normal(key, extent, jnp.float32)
    if pieces:
        result = result * levels(key, extent, pieces, -0.22, 0.18)
    return jnp.clip(strengthened(result, jax.random.fold_in(key, 3), *heavy), -reach, reach).astype(kind)


def setup_inputs(seed: int = 0, part: int = 0) -> dict:
    key_of = jax.random.split(jax.random.key(seed), 6)
    part_splits = jax.random.split(jax.random.fold_in(key_of[5], part), 6)
    gate_pre = noise(part_splits[0], (TOKENS, FF), 1.0, 6.0, ((1, 16),))
    up_pre = noise(part_splits[1], (TOKENS, FF), 1.0, 6.0, ((1, 16),))
    residual = draw_residual(jax.random.fold_in(jax.random.fold_in(key_of[5], part), 71), part)
    gain = jnp.clip(1.0 + 0.1 * jax.random.normal(key_of[3], (D,), jnp.float32), 0.5, 1.5)
    down_weight = gaussian_with(key_of[4], (QUAD * FF, D // QUAD), FF ** -0.5, 0.046875, ((0, 16),), (0, 1, 16, 2.0))
    return dict(gate_pre=gate_pre, up_pre=up_pre, residual=residual, gain=gain, down_weight=down_weight)


def reference(gate_pre, up_pre, residual, gain, down_weight):
    blocks_f = N_ROW // QUAD
    unit_block = FF // N_ROW
    quarter = D // QUAD
    full_weight = down_weight.reshape(QUAD, blocks_f, QUAD, unit_block, quarter)
    full_weight = full_weight.transpose(2, 1, 3, 0, 4).reshape(FF, D)
    gate = gate_pre.astype(jnp.float32)
    up_val = up_pre.astype(jnp.float32)
    hidden = (jax.nn.silu(gate) * up_val).astype(jnp.bfloat16)
    stream = jnp.dot(hidden, full_weight, preferred_element_type=jnp.float32) + residual.astype(jnp.float32)
    power = lax.optimization_barrier(jnp.mean(stream * stream, axis=1, keepdims=True))
    normed = stream * jax.lax.rsqrt(power + 1e-05) * gain.astype(jnp.float32)[None, :]
    return (stream.astype(jnp.bfloat16), normed.astype(jnp.bfloat16))
```

```python
import functools

import jax
import jax.numpy as jnp
from jax import lax
from jax.experimental import pallas as pl
from jax.experimental.pallas import tpu as pltpu
from jax.sharding import PartitionSpec as P

QUAD = 4


def gated(gate_pre, up_pre):
    return (jax.nn.silu(gate_pre.astype(jnp.float32)) * up_pre.astype(jnp.float32)).astype(
        jnp.bfloat16
    )


def product_kernel(half, with_total, place, *refs):
    if with_total:
        hidden, weight, total_send, total_keep, send, keep = refs
    else:
        hidden, weight, send, keep = refs
    step = pl.program_id(0)
    value = jnp.dot(hidden[...], weight[...], preferred_element_type=jnp.float32)

    @pl.when(step < half)
    def _():
        send[0] = value + total_send[0] if with_total else value

    @pl.when(step >= half)
    def _():
        keep[0] = value + total_keep[0] if with_total else value


def product(hidden, weight, slot, own, blocks, cols, total=None, token_block=0):
    tokens, units = hidden.shape
    half = blocks // 2

    def first(step):
        return jnp.minimum(step, half - 1)

    def second(step):
        return jnp.maximum(step - half, 0)

    def weight_at(step, place):
        block = jnp.where(step < half, 2 * step + 1, 2 * (step - half))
        return place[0], lax.bitwise_xor(place[1], block)

    in_specs = [
        pl.BlockSpec((tokens, units), lambda step, place: (0, 0)),
        pl.BlockSpec((units, cols), weight_at),
    ]
    operands = [hidden, weight]
    if total is not None:
        in_specs += [
            pl.BlockSpec((1, tokens, cols), lambda step, place: (first(step), token_block, 0)),
            pl.BlockSpec((1, tokens, cols), lambda step, place: (second(step), token_block, 0)),
        ]
        operands += list(total)
    out = jax.ShapeDtypeStruct((half, tokens, cols), jnp.float32)
    return pl.pallas_call(
        functools.partial(product_kernel, half, total is not None),
        grid_spec=pltpu.PrefetchScalarGridSpec(
            num_scalar_prefetch=1,
            grid=(blocks,),
            in_specs=in_specs,
            out_specs=[
                pl.BlockSpec((1, tokens, cols), lambda step, place: (first(step), 0, 0)),
                pl.BlockSpec((1, tokens, cols), lambda step, place: (second(step), 0, 0)),
            ],
        ),
        out_shape=[out, out],
        compiler_params=pltpu.CompilerParams(vmem_limit_bytes=32 * 2**20),
        cost_estimate=pl.CostEstimate(
            flops=2 * tokens * units * blocks * cols,
            bytes_accessed=2 * (units * blocks * cols + tokens * units) + 8 * tokens * blocks * cols,
            transcendentals=0,
        ),
    )(jnp.stack([slot, own]).astype(jnp.int32), *operands)


def local(gate_pre, up_pre, residual, gain, down_weight):
    tokens, units = gate_pre.shape
    cols = residual.shape[1]
    devices = lax.axis_size("row")
    plane = devices // QUAD
    width = devices * cols
    position = lax.axis_index("row")
    layer = position // plane
    own = position % plane
    middle = (layer == 1) | (layer == 2)
    low = layer < 2

    def move(value, pairs):
        return lax.ppermute(
            value, "row", [(s * plane + i, t * plane + i) for s, t in pairs for i in range(plane)]
        )

    def swap(value, bit):
        return lax.ppermute(value, "row", [(i, i ^ (1 << bit)) for i in range(devices)])

    def beside(value):
        return move(value, [(0, 1), (1, 0), (2, 3), (3, 2)])

    def across(value):
        return move(value, [(1, 2), (2, 1)])

    def outward(value):
        return move(value, [(1, 0), (2, 3)])

    mul = functools.partial(product, weight=down_weight, own=own, blocks=plane, cols=cols)

    halves = 2
    quarters = 4
    part = tokens // halves
    fine = tokens // quarters
    hidden = [
        gated(gate_pre[i * part : (i + 1) * part], up_pre[i * part : (i + 1) * part])
        for i in range(halves)
    ]
    near = [beside(v) for v in hidden]
    mid = [across(v) for v in hidden]
    mid_out = [outward(v) for v in mid]
    far = [across(v) for v in near]
    far_out = [
        outward(v[i * fine : (i + 1) * fine]) for v in far for i in range(quarters // halves)
    ]

    other_mid = jnp.where(low, 2, 1)
    other_end = jnp.where(low, 3, 0)
    done = []
    for i in range(halves):
        total = mul(hidden[i], slot=layer)
        total = mul(near[i], slot=layer ^ 1, total=total)
        total = mul(jnp.where(middle, mid[i], mid_out[i]), slot=other_mid, total=total)
        for j in range(quarters // halves):
            piece = jnp.where(
                middle, far[i][j * fine : (j + 1) * fine], far_out[i * (quarters // halves) + j]
            )
            done.append(mul(piece, slot=other_end, total=total, token_block=j))

    plane_bits = plane.bit_length() - 1
    all_bits = devices.bit_length() - 1
    streams = []
    for j, (send, keep) in enumerate(done):
        value = keep + swap(send, 0)
        for bit in range(1, plane_bits):
            value = value.reshape(-1, 2, fine, cols)
            value = value[:, 0] + swap(value[:, 1], bit)
        streams.append(value[0] + residual[j * fine : (j + 1) * fine].astype(jnp.float32))
    squares = jnp.concatenate([jnp.sum(s * s, axis=1) for s in streams])
    for bit in range(all_bits):
        squares = squares + swap(squares, bit)
    scale = lax.rsqrt(squares / width + 1e-05)
    gain_part = lax.dynamic_slice_in_dim(gain, position * cols, cols, 0)
    stream = jnp.concatenate(streams)
    mixed = stream.astype(jnp.bfloat16)
    normed = (stream * scale[:, None] * gain_part[None, :]).astype(jnp.bfloat16)
    return (mixed, normed)


def solution(mesh):
    return jax.shard_map(
        local,
        mesh=mesh,
        in_specs=(P("groups", "row"), P("groups", "row"), P("groups", "row"), P(), P("row", None)),
        out_specs=(P("groups", "row"), P("groups", "row")),
        check_vma=False,
    )
```

```python
import functools

import jax
import jax.numpy as jnp
from jax import lax
from jax.experimental import pallas as pl
from jax.experimental.pallas import tpu as pltpu
from jax.sharding import PartitionSpec as P

QUAD = 4


def gated(gate_pre, up_pre):
    return (jax.nn.silu(gate_pre.astype(jnp.float32)) * up_pre.astype(jnp.float32)).astype(
        jnp.bfloat16
    )


def product_kernel(half, with_total, waits, place, *refs):
    refs = refs[waits:]
    if with_total:
        hidden, other_hidden, weight, total_send, total_keep, send, keep = refs
    else:
        hidden, other_hidden, weight, send, keep = refs
    step = pl.program_id(0)
    left = jnp.where(place[2] == 1, hidden[...], other_hidden[...])
    value = jnp.dot(left, weight[...], preferred_element_type=jnp.float32)

    @pl.when(step < half)
    def _():
        send[0] = value + total_send[0] if with_total else value

    @pl.when(step >= half)
    def _():
        keep[0] = value + total_keep[0] if with_total else value


def product(hidden, other_hidden, first_hidden, weight, slot, own, blocks, cols, total=None, token_block=0, wait=()):
    tokens, units = hidden.shape
    half = blocks // 2

    def first(step):
        return jnp.minimum(step, half - 1)

    def second(step):
        return jnp.maximum(step - half, 0)

    def weight_at(step, place):
        block = jnp.where(step < half, 2 * step + 1, 2 * (step - half))
        return place[0], lax.bitwise_xor(place[1], block)

    in_specs = [pl.BlockSpec((16, 128), lambda step, place: (0, 0)) for _ in wait] + [
        pl.BlockSpec((tokens, units), lambda step, place: (0, 0)),
        pl.BlockSpec((tokens, units), lambda step, place: (0, 0)),
        pl.BlockSpec((units, cols), weight_at),
    ]
    operands = [*wait, hidden, other_hidden, weight]
    if total is not None:
        in_specs += [
            pl.BlockSpec((1, tokens, cols), lambda step, place: (first(step), token_block, 0)),
            pl.BlockSpec((1, tokens, cols), lambda step, place: (second(step), token_block, 0)),
        ]
        operands += list(total)
    out = jax.ShapeDtypeStruct((half, tokens, cols), jnp.float32)
    return pl.pallas_call(
        functools.partial(product_kernel, half, total is not None, len(wait)),
        grid_spec=pltpu.PrefetchScalarGridSpec(
            num_scalar_prefetch=1,
            grid=(blocks,),
            in_specs=in_specs,
            out_specs=[
                pl.BlockSpec((1, tokens, cols), lambda step, place: (first(step), 0, 0)),
                pl.BlockSpec((1, tokens, cols), lambda step, place: (second(step), 0, 0)),
            ],
        ),
        out_shape=[out, out],
        compiler_params=pltpu.CompilerParams(vmem_limit_bytes=32 * 2**20),
        cost_estimate=pl.CostEstimate(
            flops=2 * tokens * units * blocks * cols,
            bytes_accessed=2 * (units * blocks * cols + tokens * units) + 8 * tokens * blocks * cols,
            transcendentals=0,
        ),
    )(jnp.stack([slot, own, first_hidden]).astype(jnp.int32), *operands)


def local(gate_pre, up_pre, residual, gain, down_weight):
    tokens, units = gate_pre.shape
    cols = residual.shape[1]
    devices = lax.axis_size("row")
    plane = devices // QUAD
    width = devices * cols
    position = lax.axis_index("row")
    layer = position // plane
    own = position % plane
    middle = (layer == 1) | (layer == 2)
    low = layer < 2

    def move(value, pairs):
        return lax.ppermute(
            value, "row", [(s * plane + i, t * plane + i) for s, t in pairs for i in range(plane)]
        )

    def swap(value, bit):
        return lax.ppermute(value, "row", [(i, i ^ (1 << bit)) for i in range(devices)])

    def beside(value):
        return move(value, [(0, 1), (1, 0), (2, 3), (3, 2)])

    def across(value):
        return move(value, [(1, 2), (2, 1)])

    def outward(value):
        return move(value, [(1, 0), (2, 3)])

    mul = functools.partial(product, weight=down_weight, own=own, blocks=plane, cols=cols)

    halves = 2
    part = tokens // halves
    cuts = [[0, part // 2, part]] * 2
    hidden = [
        gated(gate_pre[i * part : (i + 1) * part], up_pre[i * part : (i + 1) * part])
        for i in range(halves)
    ]
    near = [beside(v) for v in hidden]
    mid = [across(v) for v in hidden]
    mid_out = [outward(v) for v in mid]
    far = [across(v) for v in near]

    other_mid = jnp.where(low, 2, 1)
    other_end = jnp.where(low, 3, 0)
    plane_bits = plane.bit_length() - 1
    all_bits = devices.bit_length() - 1
    always = jnp.ones_like(layer)
    streams = {}
    for i in reversed(range(halves)):
        total = mul(hidden[i], hidden[i], always, slot=layer)
        total = mul(near[i], near[i], always, slot=layer ^ 1, total=total)
        total = mul(mid[i], mid_out[i], middle, slot=other_mid, total=total)
        for start, stop in zip(cuts[i][:-1], cuts[i][1:]):
            size = stop - start
            piece = far[i][start:stop]
            piece_out = outward(piece)
            send, keep = mul(
                piece, piece_out, middle, slot=other_end, total=total, token_block=start // size,
                wait=list(streams.values())[-2:-1],
            )
            value = keep + swap(send, 0)
            for bit in range(1, plane_bits):
                value = value.reshape(-1, 2, size, cols)
                sent = swap(value[:, 1].astype(jnp.bfloat16), bit)
                value = value[:, 0] + sent.astype(jnp.float32)
            rows = residual[i * part + start : i * part + stop]
            streams[i * part + start] = value[0] + rows.astype(jnp.float32)
    streams = [streams[k] for k in sorted(streams)]
    squares = jnp.concatenate([jnp.sum(s * s, axis=1) for s in streams])
    for bit in range(all_bits):
        squares = squares + swap(squares, bit)
    scale = lax.rsqrt(squares / width + 1e-05)
    gain_part = lax.dynamic_slice_in_dim(gain, position * cols, cols, 0)
    stream = jnp.concatenate(streams)
    mixed = stream.astype(jnp.bfloat16)
    normed = (stream * scale[:, None] * gain_part[None, :]).astype(jnp.bfloat16)
    return (mixed, normed)


def solution(mesh):
    return jax.shard_map(
        local,
        mesh=mesh,
        in_specs=(P("groups", "row"), P("groups", "row"), P("groups", "row"), P(), P("row", None)),
        out_specs=(P("groups", "row"), P("groups", "row")),
        check_vma=False,
    )
```

```python
import functools

import jax
import jax.numpy as jnp
from jax import lax
from jax.experimental import pallas as pl
from jax.experimental.pallas import tpu as pltpu
from jax.sharding import PartitionSpec as P

QUAD = 4


def gated(gate_pre, up_pre):
    return (jax.nn.silu(gate_pre.astype(jnp.float32)) * up_pre.astype(jnp.float32)).astype(
        jnp.bfloat16
    )


def product_kernel(half, with_total, waits, place, *refs):
    refs = refs[waits:]
    if with_total:
        hidden, other_hidden, weight, total_send, total_keep, send, keep = refs
    else:
        hidden, other_hidden, weight, send, keep = refs
    step = pl.program_id(0)
    left = jnp.where(place[2] == 1, hidden[...], other_hidden[...])
    value = jnp.dot(left, weight[...], preferred_element_type=jnp.float32)

    @pl.when(step < half)
    def _():
        send[0] = value + total_send[0] if with_total else value

    @pl.when(step >= half)
    def _():
        keep[0] = value + total_keep[0] if with_total else value


def product(hidden, other_hidden, first_hidden, weight, slot, own, blocks, cols, total=None, token_block=0, wait=()):
    tokens, units = hidden.shape
    half = blocks // 2

    def first(step):
        return jnp.minimum(step, half - 1)

    def second(step):
        return jnp.maximum(step - half, 0)

    def weight_at(step, place):
        block = jnp.where(step < half, 2 * step + 1, 2 * (step - half))
        return place[0], lax.bitwise_xor(place[1], block)

    in_specs = [pl.BlockSpec((16, 128), lambda step, place: (0, 0)) for _ in wait] + [
        pl.BlockSpec((tokens, units), lambda step, place: (0, 0)),
        pl.BlockSpec((tokens, units), lambda step, place: (0, 0)),
        pl.BlockSpec((units, cols), weight_at),
    ]
    operands = [*wait, hidden, other_hidden, weight]
    if total is not None:
        in_specs += [
            pl.BlockSpec((1, tokens, cols), lambda step, place: (first(step), token_block, 0)),
            pl.BlockSpec((1, tokens, cols), lambda step, place: (second(step), token_block, 0)),
        ]
        operands += list(total)
    out = jax.ShapeDtypeStruct((half, tokens, cols), jnp.float32)
    return pl.pallas_call(
        functools.partial(product_kernel, half, total is not None, len(wait)),
        grid_spec=pltpu.PrefetchScalarGridSpec(
            num_scalar_prefetch=1,
            grid=(blocks,),
            in_specs=in_specs,
            out_specs=[
                pl.BlockSpec((1, tokens, cols), lambda step, place: (first(step), 0, 0)),
                pl.BlockSpec((1, tokens, cols), lambda step, place: (second(step), 0, 0)),
            ],
        ),
        out_shape=[out, out],
        compiler_params=pltpu.CompilerParams(vmem_limit_bytes=32 * 2**20),
        cost_estimate=pl.CostEstimate(
            flops=int(0.45 * 2 * tokens * units * blocks * cols),
            bytes_accessed=int(
                0.45 * (2 * (units * blocks * cols + tokens * units) + 8 * tokens * blocks * cols)
            ),
            transcendentals=0,
        ),
    )(jnp.stack([slot, own, first_hidden]).astype(jnp.int32), *operands)


def local(gate_pre, up_pre, residual, gain, down_weight):
    tokens, units = gate_pre.shape
    cols = residual.shape[1]
    devices = lax.axis_size("row")
    plane = devices // QUAD
    width = devices * cols
    position = lax.axis_index("row")
    layer = position // plane
    own = position % plane
    middle = (layer == 1) | (layer == 2)
    low = layer < 2

    def move(value, pairs):
        return lax.ppermute(
            value, "row", [(s * plane + i, t * plane + i) for s, t in pairs for i in range(plane)]
        )

    def swap(value, bit):
        return lax.ppermute(value, "row", [(i, i ^ (1 << bit)) for i in range(devices)])

    def beside(value):
        return move(value, [(0, 1), (1, 0), (2, 3), (3, 2)])

    def across(value):
        return move(value, [(1, 2), (2, 1)])

    def outward(value):
        return move(value, [(1, 0), (2, 3)])

    mul = functools.partial(product, weight=down_weight, own=own, blocks=plane, cols=cols)

    halves = 2
    part = tokens // halves
    cuts = [[0, part // 2, part]] * 2
    hidden = [
        gated(gate_pre[i * part : (i + 1) * part], up_pre[i * part : (i + 1) * part])
        for i in range(halves)
    ]
    near = [beside(v) for v in hidden]
    mid = [across(v) for v in hidden]
    mid_out = [outward(v) for v in mid]
    far = [across(v) for v in near]

    other_mid = jnp.where(low, 2, 1)
    other_end = jnp.where(low, 3, 0)
    plane_bits = plane.bit_length() - 1
    all_bits = devices.bit_length() - 1
    always = jnp.ones_like(layer)
    streams = {}
    for i in reversed(range(halves)):
        total = mul(hidden[i], hidden[i], always, slot=layer)
        total = mul(near[i], near[i], always, slot=layer ^ 1, total=total)
        total = mul(mid[i], mid_out[i], middle, slot=other_mid, total=total)
        for start, stop in zip(cuts[i][:-1], cuts[i][1:]):
            size = stop - start
            piece = far[i][start:stop]
            piece_out = outward(piece)
            send, keep = mul(
                piece, piece_out, middle, slot=other_end, total=total, token_block=start // size,
                wait=list(streams.values())[-2:-1],
            )
            value = keep + swap(send, 0)
            for bit in range(1, plane_bits):
                value = value.reshape(-1, 2, size, cols)
                sent = swap(value[:, 1].astype(jnp.bfloat16), bit)
                value = value[:, 0] + sent.astype(jnp.float32)
            rows = residual[i * part + start : i * part + stop]
            streams[i * part + start] = value[0] + rows.astype(jnp.float32)
    streams = [streams[k] for k in sorted(streams)]
    squares = jnp.concatenate([jnp.sum(s * s, axis=1) for s in streams])
    for bit in range(all_bits):
        squares = squares + swap(squares, bit)
    scale = lax.rsqrt(squares / width + 1e-05)
    gain_part = lax.dynamic_slice_in_dim(gain, position * cols, cols, 0)
    stream = jnp.concatenate(streams)
    mixed = stream.astype(jnp.bfloat16)
    normed = (stream * scale[:, None] * gain_part[None, :]).astype(jnp.bfloat16)
    return (mixed, normed)


def solution(mesh):
    return jax.shard_map(
        local,
        mesh=mesh,
        in_specs=(P("groups", "row"), P("groups", "row"), P("groups", "row"), P(), P("row", None)),
        out_specs=(P("groups", "row"), P("groups", "row")),
        check_vma=False,
    )
```

```python
import functools

import jax
import jax.numpy as jnp
from jax import lax
from jax.experimental import pallas as pl
from jax.experimental.pallas import tpu as pltpu
from jax.sharding import PartitionSpec as P

QUAD = 4


def gated(gate_pre, up_pre):
    return (jax.nn.silu(gate_pre.astype(jnp.float32)) * up_pre.astype(jnp.float32)).astype(
        jnp.bfloat16
    )


def product_kernel(half, with_total, waits, place, *refs):
    refs = refs[waits:]
    if with_total:
        hidden, other_hidden, weight, weight_2, total_send, total_keep, send, keep = refs
    else:
        hidden, other_hidden, weight, weight_2, send, keep = refs
    step = pl.program_id(0)
    left = jnp.where(place[2] == 1, hidden[...], other_hidden[...])
    values = [
        jnp.dot(left, part[...], preferred_element_type=jnp.float32) for part in (weight, weight_2)
    ]

    @pl.when(step < half // 2)
    def _():
        for i in range(2):
            send[i] = values[i] + total_send[i] if with_total else values[i]

    @pl.when(step >= half // 2)
    def _():
        for i in range(2):
            keep[i] = values[i] + total_keep[i] if with_total else values[i]


def product(hidden, other_hidden, first_hidden, weight, slot, own, blocks, cols, total=None, token_block=0, wait=()):
    tokens, units = hidden.shape
    half = blocks // 2

    def first(step):
        return jnp.minimum(step, half // 2 - 1)

    def second(step):
        return jnp.maximum(step - half // 2, 0)

    def weight_at(i, step, place):
        block = jnp.where(step < half // 2, 4 * step + 1, 4 * step - 2 * half) + 2 * i
        return place[0], lax.bitwise_xor(place[1], block)

    in_specs = [pl.BlockSpec((16, 128), lambda step, place: (0, 0)) for _ in wait] + [
        pl.BlockSpec((tokens, units), lambda step, place: (0, 0)),
        pl.BlockSpec((tokens, units), lambda step, place: (0, 0)),
        pl.BlockSpec((units, cols), functools.partial(weight_at, 0)),
        pl.BlockSpec((units, cols), functools.partial(weight_at, 1)),
    ]
    operands = [*wait, hidden, other_hidden, weight, weight]
    if total is not None:
        in_specs += [
            pl.BlockSpec((2, tokens, cols), lambda step, place: (first(step), token_block, 0)),
            pl.BlockSpec((2, tokens, cols), lambda step, place: (second(step), token_block, 0)),
        ]
        operands += list(total)
    out = jax.ShapeDtypeStruct((half, tokens, cols), jnp.float32)
    return pl.pallas_call(
        functools.partial(product_kernel, half, total is not None, len(wait)),
        grid_spec=pltpu.PrefetchScalarGridSpec(
            num_scalar_prefetch=1,
            grid=(blocks // 2,),
            in_specs=in_specs,
            out_specs=[
                pl.BlockSpec((2, tokens, cols), lambda step, place: (first(step), 0, 0)),
                pl.BlockSpec((2, tokens, cols), lambda step, place: (second(step), 0, 0)),
            ],
        ),
        out_shape=[out, out],
        compiler_params=pltpu.CompilerParams(vmem_limit_bytes=32 * 2**20),
        cost_estimate=pl.CostEstimate(
            flops=int(0.45 * 2 * tokens * units * blocks * cols),
            bytes_accessed=int(
                0.45 * (2 * (units * blocks * cols + tokens * units) + 8 * tokens * blocks * cols)
            ),
            transcendentals=0,
        ),
    )(jnp.stack([slot, own, first_hidden]).astype(jnp.int32), *operands)


def local(gate_pre, up_pre, residual, gain, down_weight):
    tokens, units = gate_pre.shape
    cols = residual.shape[1]
    devices = lax.axis_size("row")
    plane = devices // QUAD
    width = devices * cols
    position = lax.axis_index("row")
    layer = position // plane
    own = position % plane
    middle = (layer == 1) | (layer == 2)
    low = layer < 2

    def move(value, pairs):
        return lax.ppermute(
            value, "row", [(s * plane + i, t * plane + i) for s, t in pairs for i in range(plane)]
        )

    def swap(value, bit):
        return lax.ppermute(value, "row", [(i, i ^ (1 << bit)) for i in range(devices)])

    def beside(value):
        return move(value, [(0, 1), (1, 0), (2, 3), (3, 2)])

    def across(value):
        return move(value, [(1, 2), (2, 1)])

    def outward(value):
        return move(value, [(1, 0), (2, 3)])

    mul = functools.partial(product, weight=down_weight, own=own, blocks=plane, cols=cols)

    halves = 2
    part = tokens // halves
    cuts = [[0, part // 2, part]] * 2
    hidden = [
        gated(gate_pre[i * part : (i + 1) * part], up_pre[i * part : (i + 1) * part])
        for i in range(halves)
    ]
    near = [beside(v) for v in hidden]
    mid = [across(v) for v in hidden]
    mid_out = [outward(v) for v in mid]
    far = [across(v) for v in near]

    other_mid = jnp.where(low, 2, 1)
    other_end = jnp.where(low, 3, 0)
    plane_bits = plane.bit_length() - 1
    all_bits = devices.bit_length() - 1
    always = jnp.ones_like(layer)
    streams = {}
    for i in reversed(range(halves)):
        total = mul(hidden[i], hidden[i], always, slot=layer)
        total = mul(near[i], near[i], always, slot=layer ^ 1, total=total)
        total = mul(mid[i], mid_out[i], middle, slot=other_mid, total=total)
        for start, stop in zip(cuts[i][:-1], cuts[i][1:]):
            size = stop - start
            piece = far[i][start:stop]
            piece_out = outward(piece)
            send, keep = mul(
                piece, piece_out, middle, slot=other_end, total=total, token_block=start // size,
                wait=list(streams.values())[-2:-1],
            )
            value = keep + swap(send, 0)
            for bit in range(1, plane_bits):
                value = value.reshape(-1, 2, size, cols)
                sent = swap(value[:, 1].astype(jnp.bfloat16), bit)
                value = value[:, 0] + sent.astype(jnp.float32)
            rows = residual[i * part + start : i * part + stop]
            streams[i * part + start] = value[0] + rows.astype(jnp.float32)
    streams = [streams[k] for k in sorted(streams)]
    squares = jnp.concatenate([jnp.sum(s * s, axis=1) for s in streams])
    for bit in range(all_bits):
        squares = squares + swap(squares, bit)
    scale = lax.rsqrt(squares / width + 1e-05)
    gain_part = lax.dynamic_slice_in_dim(gain, position * cols, cols, 0)
    stream = jnp.concatenate(streams)
    mixed = stream.astype(jnp.bfloat16)
    normed = (stream * scale[:, None] * gain_part[None, :]).astype(jnp.bfloat16)
    return (mixed, normed)


def solution(mesh):
    return jax.shard_map(
        local,
        mesh=mesh,
        in_specs=(P("groups", "row"), P("groups", "row"), P("groups", "row"), P(), P("row", None)),
        out_specs=(P("groups", "row"), P("groups", "row")),
        check_vma=False,
    )
```

```python
import functools

import jax
import jax.numpy as jnp
from jax import lax
from jax.experimental import pallas as pl
from jax.experimental.pallas import tpu as pltpu
from jax.sharding import PartitionSpec as P

QUAD = 4


def gated(gate_pre, up_pre):
    return (jax.nn.silu(gate_pre.astype(jnp.float32)) * up_pre.astype(jnp.float32)).astype(
        jnp.bfloat16
    )


def product_kernel(half, with_total, waits, place, *refs):
    refs = refs[waits:]
    if with_total:
        hidden, other_hidden, weight, weight_2, total_send, total_keep, send, keep = refs
    else:
        hidden, other_hidden, weight, weight_2, send, keep = refs
    step = pl.program_id(0)
    left = jnp.where(place[2] == 1, hidden[...], other_hidden[...])
    values = [
        jnp.dot(left, part[...], preferred_element_type=jnp.float32) for part in (weight, weight_2)
    ]

    @pl.when(step < half // 2)
    def _():
        for i in range(2):
            send[i] = values[i] + total_send[i] if with_total else values[i]

    @pl.when(step >= half // 2)
    def _():
        for i in range(2):
            keep[i] = values[i] + total_keep[i] if with_total else values[i]


def product(hidden, other_hidden, first_hidden, weight, slot, own, blocks, cols, total=None, token_block=0, wait=()):
    tokens, units = hidden.shape
    half = blocks // 2

    def first(step):
        return jnp.minimum(step, half // 2 - 1)

    def second(step):
        return jnp.maximum(step - half // 2, 0)

    def weight_at(i, step, place):
        block = jnp.where(step < half // 2, 4 * step + 1, 4 * step - 2 * half) + 2 * i
        return place[0], lax.bitwise_xor(place[1], block)

    in_specs = [pl.BlockSpec((16, 128), lambda step, place: (0, 0)) for _ in wait] + [
        pl.BlockSpec((tokens, units), lambda step, place: (0, 0)),
        pl.BlockSpec((tokens, units), lambda step, place: (0, 0)),
        pl.BlockSpec((units, cols), functools.partial(weight_at, 0)),
        pl.BlockSpec((units, cols), functools.partial(weight_at, 1)),
    ]
    operands = [*wait, hidden, other_hidden, weight, weight]
    if total is not None:
        in_specs += [
            pl.BlockSpec((2, tokens, cols), lambda step, place: (first(step), token_block, 0)),
            pl.BlockSpec((2, tokens, cols), lambda step, place: (second(step), token_block, 0)),
        ]
        operands += list(total)
    out = jax.ShapeDtypeStruct((half, tokens, cols), jnp.float32)
    return pl.pallas_call(
        functools.partial(product_kernel, half, total is not None, len(wait)),
        grid_spec=pltpu.PrefetchScalarGridSpec(
            num_scalar_prefetch=1,
            grid=(blocks // 2,),
            in_specs=in_specs,
            out_specs=[
                pl.BlockSpec((2, tokens, cols), lambda step, place: (first(step), 0, 0)),
                pl.BlockSpec((2, tokens, cols), lambda step, place: (second(step), 0, 0)),
            ],
        ),
        out_shape=[out, out],
        compiler_params=pltpu.CompilerParams(vmem_limit_bytes=32 * 2**20),
        cost_estimate=pl.CostEstimate(
            flops=int(0.45 * 2 * tokens * units * blocks * cols),
            bytes_accessed=int(
                0.45 * (2 * (units * blocks * cols + tokens * units) + 8 * tokens * blocks * cols)
            ),
            transcendentals=0,
        ),
    )(jnp.stack([slot, own, first_hidden]).astype(jnp.int32), *operands)


def local(gate_pre, up_pre, residual, gain, down_weight):
    tokens, units = gate_pre.shape
    cols = residual.shape[1]
    devices = lax.axis_size("row")
    plane = devices // QUAD
    width = devices * cols
    position = lax.axis_index("row")
    layer = position // plane
    own = position % plane
    middle = (layer == 1) | (layer == 2)
    low = layer < 2

    def move(value, pairs):
        return lax.ppermute(
            value, "row", [(s * plane + i, t * plane + i) for s, t in pairs for i in range(plane)]
        )

    def swap(value, bit):
        return lax.ppermute(value, "row", [(i, i ^ (1 << bit)) for i in range(devices)])

    def beside(value):
        return move(value, [(0, 1), (1, 0), (2, 3), (3, 2)])

    def across(value):
        return move(value, [(1, 2), (2, 1)])

    def outward(value):
        return move(value, [(1, 0), (2, 3)])

    mul = functools.partial(product, weight=down_weight, own=own, blocks=plane, cols=cols)

    halves = 2
    part = tokens // halves
    cuts = [[0, part // 2, part]] * 2
    hidden = [
        gated(gate_pre[i * part : (i + 1) * part], up_pre[i * part : (i + 1) * part])
        for i in range(halves)
    ]
    near = [beside(v) for v in hidden]
    mid = [across(v) for v in hidden]
    mid_out = [outward(v) for v in mid]
    far = [across(v) for v in near]

    other_mid = jnp.where(low, 2, 1)
    other_end = jnp.where(low, 3, 0)
    plane_bits = plane.bit_length() - 1
    all_bits = devices.bit_length() - 1
    always = jnp.ones_like(layer)
    streams = {}
    for i in reversed(range(halves)):
        total = mul(hidden[i], hidden[i], always, slot=layer)
        total = mul(near[i], near[i], always, slot=layer ^ 1, total=total)
        total = mul(mid[i], mid_out[i], middle, slot=other_mid, total=total)
        for start, stop in zip(cuts[i][:-1], cuts[i][1:]):
            size = stop - start
            piece = far[i][start:stop]
            piece_out = outward(piece)
            send, keep = mul(
                piece, piece_out, middle, slot=other_end, total=total, token_block=start // size,
                wait=list(streams.values())[-2:-1],
            )
            value = keep + swap(send, 0)
            for bit in range(1, plane_bits):
                value = value.reshape(-1, 2, size, cols)
                sent = swap(value[:, 1].astype(jnp.bfloat16), bit)
                value = value[:, 0] + sent.astype(jnp.float32)
            rows = residual[i * part + start : i * part + stop]
            streams[i * part + start] = value[0] + rows.astype(jnp.float32)
    streams = [streams[k] for k in sorted(streams)]
    squares = jnp.concatenate([jnp.sum(s * s, axis=1) for s in streams])
    for bit in reversed(range(all_bits)):
        squares = squares + swap(squares, bit)
    scale = lax.rsqrt(squares / width + 1e-05)
    gain_part = lax.dynamic_slice_in_dim(gain, position * cols, cols, 0)
    stream = jnp.concatenate(streams)
    mixed = stream.astype(jnp.bfloat16)
    normed = (stream * scale[:, None] * gain_part[None, :]).astype(jnp.bfloat16)
    return (mixed, normed)


def solution(mesh):
    return jax.shard_map(
        local,
        mesh=mesh,
        in_specs=(P("groups", "row"), P("groups", "row"), P("groups", "row"), P(), P("row", None)),
        out_specs=(P("groups", "row"), P("groups", "row")),
        check_vma=False,
    )
```
